256 devices in a mesh: dp: 8 (over z), slab: 2 (over core), filt: 16 (over y, x).
Axes of the slice: x: 4, y: 4, z: 8, core: 2. Of those that a mesh axis runs over, the one named last changes fastest.
Arguments:
- volume: bfloat16 [512, 16, 128, 128], P('dp', 'slab', 'filt'), parts along dimension 0, may hold values from -6 to 6
- first_weight: bfloat16 [27, 64, 64], replicated, may hold values from -0.15625 to 0.15625
- first_bias: float32 [64], replicated, may hold values from -3 to 3
- second_weight: bfloat16 [27, 64, 64], replicated, may hold values from -0.15625 to 0.15625
- second_bias: float32 [64], replicated, may hold values from -3 to 3
- down_weight: bfloat16 [8, 64, 64], replicated, may hold values from -0.25 to 0.25
- down_bias: float32 [64], replicated, may hold values from -3 to 3
Outputs:
- skip_field: bfloat16 [512, 16, 128, 128], P('dp', 'slab', 'filt'), parts along dimension 0
- coarse_field: bfloat16 [512, 8, 4096], P('dp', 'slab', 'filt'), parts along dimension 0
The draws below stay inside these ranges and needn't reach their ends.
There are 8 independent parts, one for each index of `dp`. The reference program is written for one: setup_inputs(seed, part) draws one part's arguments, and reference() takes and returns one part's arrays. A program takes and returns all parts, laid end to end along the dimension named above; an argument that names none is the same for every part. Nothing has to cross between parts.
All inputs are finite; a program needn't handle non-finite values.
Results may differ from the reference program's by a relative error of at most 0.0052.
Values may be sent and summed in bfloat16 or wider, within the bound.
No kernel may reach another device: no remote copies, remote signals or barrier semaphores. Data moves between devices by JAX's collectives and lax.ppermute only.
A program may use at most 64 MiB of HBM per device.

```python
import jax
import jax.numpy as jnp
from jax import lax

C = 64
X = 128
NZ = 16
NY = 128


def steps_of(key, dims, pieces, least, top_value):
    def one(dim, parts):
        draws = jax.random.uniform(jax.random.fold_in(jax.random.fold_in(key, 6), dim), (parts,), jnp.float32, least / len(pieces), top_value / len(pieces))
        return jnp.repeat(jnp.exp(draws), dims[dim] // parts).reshape((-1,) + (1,) * (len(dims) - dim - 1))

    factor_of = one(*pieces[0])
    for cut in pieces[1:]:
        factor_of = factor_of * one(*cut)
    return factor_of


def centred(own_key, dims, scale, limit, shards=(), kind=jnp.bfloat16):
    array = jax.random.normal(own_key, dims, jnp.float32) * scale
    if len(shards) > 0:
        array = steps_of(own_key, dims, shards, -0.22, 0.18) * array
    return jnp.clip(array, min=-limit, max=limit).astype(kind)


def setup_inputs(seed: int = 0, part: int = 0) -> dict:
    key_of = jax.random.split(jax.random.key(seed), 8)
    own_keys = jax.random.split(jax.random.fold_in(key_of[7], part), 8)
    volume = centred(own_keys[0], (C, NZ, NY, X), 1.0, 6.0, ((1, 2), (2, 16)))
    first_weight = centred(key_of[1], (27, C, C), (27 * C) ** -0.5, 0.15625)
    first_bias = centred(key_of[2], (C,), 0.5, 3.0, (), jnp.float32)
    second_weight = centred(key_of[3], (27, C, C), (27 * C) ** -0.5, 0.15625)
    second_bias = centred(key_of[4], (C,), 0.5, 3.0, (), jnp.float32)
    down_weight = centred(key_of[5], (8, C, C), (8 * C) ** -0.5, 0.25)
    down_bias = centred(key_of[6], (C,), 0.5, 3.0, (), jnp.float32)
    return dict(volume=volume, first_weight=first_weight, first_bias=first_bias, second_weight=second_weight, second_bias=second_bias, down_weight=down_weight, down_bias=down_bias)


def leaky_relu(values):
    return jnp.where(values > 0, values, 0.01 * values)


def conv_layer(source, kernel, offsets):
    chans = source.shape[0]
    padded = jnp.pad(source, ((0, 0), (1, 1), (1, 1), (1, 1)), mode="wrap")
    stencil = kernel.reshape(3, 3, 3, chans, kernel.shape[2])
    running = lax.conv_general_dilated(padded[None], stencil, (1, 1, 1), "VALID", dimension_numbers=("NCDHW", "DHWIO", "NCDHW"), preferred_element_type=jnp.float32)[0]
    result = leaky_relu(running + offsets[:, None, None, None])
    return result.astype(jnp.bfloat16)


def reference(volume, first_weight, first_bias, second_weight, second_bias, down_weight, down_bias):
    hidden = conv_layer(volume, first_weight, first_bias)
    skip_field = conv_layer(hidden, second_weight, second_bias)
    chans, planes, cells_y, cells_x = skip_field.shape
    stencil = down_weight.reshape(2, 2, 2, chans, down_weight.shape[2])
    running = lax.conv_general_dilated(skip_field[None], stencil, (2, 2, 2), "VALID", dimension_numbers=("NCDHW", "DHWIO", "NCDHW"), preferred_element_type=jnp.float32)[0]
    coarse = leaky_relu(running + down_bias[:, None, None, None]).astype(jnp.bfloat16)
    coarse_field = coarse.reshape(down_weight.shape[2], planes // 2, (cells_y // 2) * (cells_x // 2))
    return skip_field, coarse_field
```

```python
import jax
import jax.numpy as jnp
from jax import lax
from jax.experimental import pallas as pl
from jax.experimental.pallas import tpu as pltpu
from jax.sharding import PartitionSpec as P

BF = jnp.bfloat16
F32 = jnp.float32
WHOLE = pl.BlockSpec(memory_space=pltpu.VMEM)
TAPS = 9 * 64


def shape(*dims, kind=BF):
    return jax.ShapeDtypeStruct(dims, kind)


def kernel_call(body, outs, scratch, flops, name, *operands):
    size = lambda s: s.size * s.dtype.itemsize
    moved = sum(size(s) for s in operands) + sum(size(s) for s in outs)
    return pl.pallas_call(
        body,
        name=name,
        out_shape=outs,
        in_specs=[WHOLE] * len(operands),
        out_specs=[WHOLE] * len(outs),
        scratch_shapes=scratch,
        compiler_params=pltpu.CompilerParams(vmem_limit_bytes=28 * 2**20),
        cost_estimate=pl.CostEstimate(flops=flops, bytes_accessed=moved, transcendentals=0),
    )(*operands)


def lrelu(values):
    return jnp.maximum(values, 0.01 * values)


def shifted(dst, z, y, row):
    dst[z, y, 0:64] = pltpu.roll(row, 1, 1)
    dst[z, y, 64:128] = row
    dst[z, y, 128:192] = pltpu.roll(row, 127, 1)


def conv_pair(src, z, rows, weight, bias):
    cells = jnp.concatenate([src[z : z + 4, y : y + 3].reshape(4 * TAPS, 128) for y in rows], axis=1)
    sums = jnp.dot(weight[...], cells, preferred_element_type=F32)
    return lrelu(sums + bias[...]).astype(BF)


def split_kernel(vol, own, up, down, planes):
    for i, z in enumerate((6, 7, 0, 1, 2, 3, 4, 5)):
        rows = jnp.swapaxes(vol[:, z], 0, 1)
        own[z] = rows
        if i < 4:
            planes[i] = rows
        down[z] = rows[0:2]
        up[z] = rows[6:8]


def weight_kernel(first, first_bias, second, second_bias, third, third_bias, a1, a2, ad, b1, b2, bd, pick):
    eye = (lax.broadcasted_iota(jnp.int32, (64, 64), 0) == lax.broadcasted_iota(jnp.int32, (64, 64), 1))
    unit = eye.astype(BF)

    def flipped(rows):
        return lax.dot_general(unit, rows, (((1,), (1,)), ((), ())), preferred_element_type=F32).astype(BF)

    def column(bias):
        spread = jnp.where(eye, jnp.broadcast_to(bias[...].reshape(1, 64), (64, 64)), 0.0)
        return jnp.broadcast_to(jnp.sum(spread, axis=1, keepdims=True), (64, 256))

    blank = jnp.zeros((TAPS, 64), BF)
    for source, dest in ((first, a1), (second, a2)):
        rows = source[...].reshape(3 * TAPS, 64)
        dest[0:64] = flipped(jnp.concatenate([rows, blank], axis=0))
        dest[64:128] = flipped(jnp.concatenate([blank, rows], axis=0))
    ad[...] = flipped(third[...].reshape(512, 64))
    for source, dest in ((first_bias, b1), (second_bias, b2)):
        spread = column(source)
        dest[0:64] = spread
        dest[64:128] = spread
    bd[...] = column(third_bias)
    src = lax.broadcasted_iota(jnp.int32, (256, 256), 0)
    dst = lax.broadcasted_iota(jnp.int32, (256, 256), 1)
    half, cell = (dst // 64) % 2, dst % 64
    pick[...] = (src == half * 128 + 2 * cell + dst // 128).astype(F32).astype(BF)


def inner_kernel(own, planes, a1, b1, a2, b2, hidden, skip, vs, hs):
    for z in range(12):
        for y in range(8):
            row = own[z - 2, y] if 2 <= z < 10 else planes[z if z < 2 else z - 8, y]
            shifted(vs, z, y, row)
    for z in range(0, 10, 2):
        for y in range(0, 6, 2):
            out = conv_pair(vs, z, (y, y + 1), a1, b1)
            for i in range(2):
                for j in range(2):
                    row = out[64 * i : 64 * i + 64, 128 * j : 128 * j + 128]
                    shifted(hs, z + i, y + j, row)
                    place = {0: 0, 1: 1, 4: 2, 5: 3}.get(y + j)
                    if place is not None:
                        hidden[z + i, place] = row
    for z in range(0, 8, 2):
        for y in range(0, 4, 2):
            out = conv_pair(hs, z, (y, y + 1), a2, b2)
            for i in range(2):
                for j in range(2):
                    skip[z + i, y + j] = out[64 * i : 64 * i + 64, 128 * j : 128 * j + 128]


def outer_kernel(own, planes, above, below, corner_above, corner_below, hidden, mid, a1, b1, a2, b2, ad, bd, pick, skip, coarse, vs, hs, rows_out, cells):
    def source(z, y):
        if z < 2 or z >= 10:
            k = z if z < 2 else z - 8
            if y < 0:
                return corner_above[k, y + 2]
            if y >= 8:
                return corner_below[k, y - 8]
            return planes[k, y]
        if y < 0:
            return above[z - 2, y + 2]
        if y >= 8:
            return below[z - 2, y - 8]
        return own[z - 2, y]

    for strip in range(2):
        for z in range(12):
            for y in range(4):
                shifted(vs.at[strip], z, y, source(z, y - 2 if strip == 0 else y + 6))
    for strip in range(2):
        for z in range(10):
            for y in range(2):
                shifted(hs.at[strip], z, y + 2 * (1 - strip), hidden[z, 2 * strip + y])
    for strip in range(2):
        for z in range(0, 10, 2):
            out = conv_pair(vs.at[strip], z, (0, 1), a1, b1)
            for i in range(2):
                for j in range(2):
                    shifted(hs.at[strip], z + i, j + 2 * strip, out[64 * i : 64 * i + 64, 128 * j : 128 * j + 128])
    for z in range(8):
        for y in range(4):
            rows_out[z, y + 2] = mid[z, y]
    for strip in range(2):
        for z in range(0, 8, 2):
            out = conv_pair(hs.at[strip], z, (0, 1), a2, b2)
            for i in range(2):
                for j in range(2):
                    rows_out[z + i, 6 * strip + j] = out[64 * i : 64 * i + 64, 128 * j : 128 * j + 128]
    for z in range(8):
        skip[:, z] = jnp.swapaxes(rows_out[z], 0, 1)
    for z in range(8):
        for y in range(2):
            pair = rows_out[z, 4 * y : 4 * y + 4].reshape(256, 128)
            wide = jnp.concatenate([pair[0:128], pair[128:256]], axis=1)
            chosen = jnp.dot(wide, pick[...], preferred_element_type=F32).astype(BF)
            for p in range(2):
                for q in range(2):
                    cells[z, 2 * p + q, :, 128 * y : 128 * y + 128] = chosen[64 * p : 64 * p + 64, 128 * q : 128 * q + 128]
    found = []
    for z in range(4):
        sums = jnp.dot(ad[...], cells[2 * z : 2 * z + 2].reshape(512, 256), preferred_element_type=F32)
        found.append(lrelu(sums + bd[...]).astype(BF))
    for z in range(4):
        coarse[:, z] = found[z]


def per_device(volume, first_weight, first_bias, second_weight, second_bias, down_weight, down_bias):
    peers = lax.axis_size("filt")
    upward = [(i, (i + 1) % peers) for i in range(peers)]
    downward = [(j, i) for i, j in upward]
    swap = [(0, 1), (1, 0)]
    own, up, down, planes = kernel_call(
        split_kernel,
        [shape(8, 8, 64, 128), shape(8, 2, 64, 128), shape(8, 2, 64, 128), shape(4, 8, 64, 128)],
        [], 0, "split", volume,
    )
    planes = lax.ppermute(planes, "slab", swap)
    above = lax.ppermute(up, "filt", upward)
    below = lax.ppermute(down, "filt", downward)
    a1, a2, ad, b1, b2, bd, pick = kernel_call(
        weight_kernel,
        [shape(128, 4 * TAPS), shape(128, 4 * TAPS), shape(64, 512), shape(128, 256, kind=F32), shape(128, 256, kind=F32), shape(64, 256, kind=F32), shape(256, 256)],
        [], 10**8, "weights", first_weight, first_bias, second_weight, second_bias, down_weight, down_bias,
    )
    hidden, mid = kernel_call(
        inner_kernel,
        [shape(10, 4, 64, 128), shape(8, 4, 64, 128)],
        [pltpu.VMEM((12, 8, 192, 128), BF), pltpu.VMEM((10, 6, 192, 128), BF)],
        4 * 10**9, "inner", own, planes, a1, b1, a2, b2,
    )
    edges = lambda rows: jnp.concatenate([rows[6:8], rows[0:2]], axis=0)
    corner_above = lax.ppermute(edges(above), "slab", swap)
    corner_below = lax.ppermute(edges(below), "slab", swap)
    return kernel_call(
        outer_kernel,
        [shape(64, 8, 8, 128), shape(64, 4, 256)],
        [pltpu.VMEM((2, 12, 4, 192, 128), BF), pltpu.VMEM((2, 10, 4, 192, 128), BF), pltpu.VMEM((8, 8, 64, 128), BF), pltpu.VMEM((8, 4, 64, 256), BF)],
        4 * 10**9, "outer", own, planes, above, below, corner_above, corner_below, hidden, mid, a1, b1, a2, b2, ad, bd, pick,
    )


def solution(mesh):
    placed = (P("dp", "slab", "filt", None), P(), P(), P(), P(), P(), P())
    return jax.shard_map(
        lambda *args: tuple(per_device(*args)),
        mesh=mesh,
        in_specs=placed,
        out_specs=(P("dp", "slab", "filt", None), P("dp", "slab", "filt")),
        check_vma=False,
    )
```

```python
import jax
import jax.numpy as jnp
from jax import lax
from jax.experimental import pallas as pl
from jax.experimental.pallas import tpu as pltpu
from jax.sharding import PartitionSpec as P

BF = jnp.bfloat16
F32 = jnp.float32
VMEM = pl.BlockSpec(memory_space=pltpu.VMEM)
ANY = pl.BlockSpec(memory_space=pltpu.HBM)
TAPS = 9 * 64


def shape(*dims, kind=BF):
    return jax.ShapeDtypeStruct(dims, kind)


def kernel_call(body, name, flops, operands, outs, scratch=(), far_in=(), far_out=()):
    size = lambda s: s.size * s.dtype.itemsize
    moved = sum(size(s) for s in operands) + sum(size(s) for s in outs)
    return pl.pallas_call(
        body,
        name=name,
        out_shape=outs,
        in_specs=[ANY if i in far_in else VMEM for i in range(len(operands))],
        out_specs=[ANY if i in far_out else VMEM for i in range(len(outs))],
        scratch_shapes=list(scratch),
        compiler_params=pltpu.CompilerParams(vmem_limit_bytes=28 * 2**20),
        cost_estimate=pl.CostEstimate(flops=flops, bytes_accessed=moved, transcendentals=0),
    )(*operands)


def lrelu(values):
    return jnp.maximum(values, 0.01 * values)


def is_even():
    return lax.rem(lax.axis_index("filt"), 2) == 0


def shifted(dst, row):
    dst[0:64] = pltpu.roll(row, 1, 1)
    dst[64:128] = row
    dst[128:192] = pltpu.roll(row, 127, 1)


def conv_pair(block, z, rows, weight, bias):
    cells = jnp.concatenate(
        [
            jnp.concatenate([block(z + d, y + p)[...] for d in (-1, 0, 1, 2) for p in (-1, 0, 1)], axis=0)
            for y in rows
        ],
        axis=1,
    )
    sums = jnp.dot(weight[...], cells, preferred_element_type=F32)
    out = lrelu(sums + bias[...]).astype(BF)
    return [(z + i, y, out[64 * i : 64 * i + 64, 128 * j : 128 * j + 128]) for i in range(2) for j, y in enumerate(rows)]


def split_kernel(vol, w0, w1, w2, w3, w4, w5, own, first, second, planes, v0, v1, v2, v3, v4, v5, held, sems):
    order = (6, 7, 0, 1, 2, 3, 4, 5)
    copies = [pltpu.make_async_copy(vol.at[:, z], held.at[z], sems.at[z]) for z in order]
    copies += [
        pltpu.make_async_copy(a, b, sems.at[8 + i])
        for i, (a, b) in enumerate(((w0, v0), (w1, v1), (w2, v2), (w3, v3), (w4, v4), (w5, v5)))
    ]
    for copy in copies:
        copy.start()
    even = is_even()
    for i, z in enumerate(order):
        copies[i].wait()
        rows = jnp.swapaxes(held[z], 0, 1)
        own[z] = rows
        if i < 4:
            planes[i] = rows
        first[z] = jnp.where(even, rows[6:8], rows[0:2])
        second[z] = jnp.where(even, rows[0:2], rows[6:8])
    for copy in copies[8:]:
        copy.wait()


def weight_kernel(first, first_bias, second, second_bias, third, third_bias, a1, a2, ad, b1, b2, bd, pick):
    eye = lax.broadcasted_iota(jnp.int32, (64, 64), 0) == lax.broadcasted_iota(jnp.int32, (64, 64), 1)
    unit = eye.astype(BF)

    def flipped(rows):
        return lax.dot_general(unit, rows, (((1,), (1,)), ((), ())), preferred_element_type=F32).astype(BF)

    def column(bias):
        spread = jnp.where(eye, jnp.broadcast_to(bias[...].reshape(1, 64), (64, 64)), 0.0)
        return jnp.broadcast_to(jnp.sum(spread, axis=1, keepdims=True), (64, 256))

    blank = jnp.zeros((TAPS, 64), BF)
    for source, dest in ((first, a1), (second, a2)):
        rows = source[...].reshape(3 * TAPS, 64)
        dest[0:64] = flipped(jnp.concatenate([rows, blank], axis=0))
        dest[64:128] = flipped(jnp.concatenate([blank, rows], axis=0))
    ad[...] = flipped(third[...].reshape(512, 64))
    for source, dest in ((first_bias, b1), (second_bias, b2)):
        spread = column(source)
        dest[0:64] = spread
        dest[64:128] = spread
    bd[...] = column(third_bias)
    src = lax.broadcasted_iota(jnp.int32, (256, 256), 0)
    dst = lax.broadcasted_iota(jnp.int32, (256, 256), 1)
    half, cell = (dst // 64) % 2, dst % 64
    pick[...] = (src == half * 128 + 2 * cell + dst // 128).astype(F32).astype(BF)


EDGE = {0: 0, 1: 1, 6: 2, 7: 3}
FAR = {-2: 0, -1: 1, 8: 2, 9: 3}
KEPT = {1: 0, 2: 1, 5: 2, 6: 3}
NEW = {-1: 0, 0: 1, 7: 2, 8: 3}
CORNER = {-2: 0, -1: 1, 8: 2, 9: 3}
SIDE = {-1: 0, 0: 1, 7: 2, 8: 3}


def inner_kernel(own, planes, a1, b1, a2, b2, edge, kept, skip, vs, hs):
    def spot(z, y):
        return edge.at[z + 2, EDGE[y]] if y in EDGE else vs.at[z + 2, y - 2]

    def hidden(z, y):
        return kept.at[z + 1, KEPT[y]] if y in KEPT else hs.at[z + 1, y - 3]

    for z in range(-2, 10):
        for y in range(8):
            shifted(spot(z, y), own[z, y] if 0 <= z < 8 else planes[CORNER[z], y])
    for z in range(-1, 9, 2):
        for y in (1, 3, 5):
            for zo, yo, row in conv_pair(spot, z, (y, y + 1), a1, b1):
                shifted(hidden(zo, yo), row)
    for z in range(0, 8, 2):
        for y in (2, 4):
            for zo, yo, row in conv_pair(hidden, z, (y, y + 1), a2, b2):
                skip[zo, yo - 2] = row


def middle_kernel(first, second, edge, kept, a1, b1, a2, b2, far, fresh, skip):
    even = is_even()
    for z in range(8):
        for i in range(2):
            shifted(far.at[z, i], jnp.where(even, second[z, i], first[z, i]))
            shifted(far.at[z, 2 + i], jnp.where(even, first[z, i], second[z, i]))

    def spot(z, y):
        return edge.at[z + 2, EDGE[y]] if y in EDGE else far.at[z, FAR[y]]

    def hidden(z, y):
        return kept.at[z + 1, KEPT[y]] if y in KEPT else fresh.at[z - 1, NEW[y]]

    for z in (1, 3, 5):
        for y in (-1, 7):
            for zo, yo, row in conv_pair(spot, z, (y, y + 1), a1, b1):
                shifted(hidden(zo, yo), row)
    for z in (2, 4):
        for y in (0, 6):
            for zo, yo, row in conv_pair(hidden, z, (y, y + 1), a2, b2):
                skip[zo - 2, EDGE[yo]] = row


def outer_kernel(
    corners, edge, far, kept, fresh, mid, part, a1, b1, a2, b2, ad, bd, pick, skip, coarse, near, side, ends, cells, held, sems
):
    even = is_even()
    for k in range(4):
        for i in range(2):
            shifted(near.at[k, i], jnp.where(even, corners[1, k, i], corners[0, k, i]))
            shifted(near.at[k, 2 + i], jnp.where(even, corners[0, k, i], corners[1, k, i]))

    def spot(z, y):
        if y in EDGE:
            return edge.at[z + 2, EDGE[y]]
        return near.at[CORNER[z], FAR[y]] if z in CORNER else far.at[z, FAR[y]]

    def hidden(z, y):
        if y in KEPT:
            return kept.at[z + 1, KEPT[y]]
        return side.at[SIDE[z], NEW[y]] if z in SIDE else fresh.at[z - 1, NEW[y]]

    def row_of(z, y):
        if y not in EDGE:
            return mid.at[z, y - 2]
        return part.at[z - 2, EDGE[y]] if 2 <= z < 6 else ends.at[z if z < 2 else z - 4, EDGE[y]]

    copies = []

    def finish(z):
        rows = jnp.stack([row_of(z, y)[...] for y in range(8)], axis=0)
        held[z] = jnp.swapaxes(rows, 0, 1)
        copy = pltpu.make_async_copy(held.at[z], skip.at[:, z], sems.at[z])
        copy.start()
        copies.append(copy)
        for y in range(2):
            wide = jnp.concatenate(
                [jnp.concatenate([rows[4 * y + j], rows[4 * y + j + 1]], axis=0) for j in (0, 2)], axis=1
            )
            chosen = jnp.dot(wide, pick[...], preferred_element_type=F32).astype(BF)
            for p in range(2):
                for q in range(2):
                    cells[z, 2 * p + q, :, 128 * y : 128 * y + 128] = chosen[64 * p : 64 * p + 64, 128 * q : 128 * q + 128]

    for z in range(2, 6):
        finish(z)
    for z in (-1, 7):
        for y in (-1, 7):
            for zo, yo, row in conv_pair(spot, z, (y, y + 1), a1, b1):
                shifted(hidden(zo, yo), row)
    for z in (0, 6):
        for y in (0, 6):
            for zo, yo, row in conv_pair(hidden, z, (y, y + 1), a2, b2):
                row_of(zo, yo)[...] = row
        finish(z)
        finish(z + 1)
    found = []
    for z in range(4):
        sums = jnp.dot(ad[...], cells[2 * z : 2 * z + 2].reshape(512, 256), preferred_element_type=F32)
        found.append(lrelu(sums + bd[...]).astype(BF))
    for z in range(4):
        coarse[:, z] = found[z]
    for copy in copies:
        copy.wait()


def per_device(volume, first_weight, first_bias, second_weight, second_bias, down_weight, down_bias):
    peers = lax.axis_size("filt")

    def pairs(begin):
        ways = [(i, (i + 1) % peers) for i in range(begin, peers, 2)]
        return ways + [(j, i) for i, j in ways]

    swap = [(0, 1), (1, 0)]
    raw = [first_weight, first_bias, second_weight, second_bias, down_weight, down_bias]
    operands = [pltpu.with_memory_space_constraint(a, pltpu.HBM) for a in [volume] + raw]
    own, first, second, planes, *raw = kernel_call(
        split_kernel, "split", 0, operands,
        [shape(8, 8, 64, 128), shape(8, 2, 64, 128), shape(8, 2, 64, 128), shape(4, 8, 64, 128)]
        + [shape(*a.shape, kind=a.dtype) for a in raw],
        [pltpu.VMEM((8, 64, 8, 128), BF), pltpu.SemaphoreType.DMA((14,))], far_in=range(7),
    )
    second = lax.ppermute(second, "filt", pairs(1))
    first = lax.ppermute(first, "filt", pairs(0))
    planes = lax.ppermute(planes, "slab", swap)
    a1, a2, ad, b1, b2, bd, pick = kernel_call(
        weight_kernel, "weights", 10**8,
        raw,
        [shape(128, 4 * TAPS), shape(128, 4 * TAPS), shape(64, 512), shape(128, 256, kind=F32), shape(128, 256, kind=F32), shape(64, 256, kind=F32), shape(256, 256)],
    )
    edge, kept, mid = kernel_call(
        inner_kernel, "inner", 4 * 10**9, [own, planes, a1, b1, a2, b2],
        [shape(12, 4, 192, 128), shape(10, 4, 192, 128), shape(8, 4, 64, 128)],
        [pltpu.VMEM((12, 4, 192, 128), BF), pltpu.VMEM((10, 2, 192, 128), BF)],
    )
    first, second, mid = lax.optimization_barrier((first, second, mid))
    edges = jnp.stack([jnp.concatenate([rows[6:8], rows[0:2]], axis=0) for rows in (first, second)], axis=0)
    corners = lax.ppermute(edges, "slab", swap)
    far, fresh, part = kernel_call(
        middle_kernel, "middle", 2 * 10**9, [first, second, edge, kept, a1, b1, a2, b2],
        [shape(8, 4, 192, 128), shape(6, 4, 192, 128), shape(4, 4, 64, 128)],
    )
    return kernel_call(
        outer_kernel, "outer", 2 * 10**9, [corners, edge, far, kept, fresh, mid, part, a1, b1, a2, b2, ad, bd, pick],
        [shape(64, 8, 8, 128), shape(64, 4, 256)],
        [
            pltpu.VMEM((4, 4, 192, 128), BF),
            pltpu.VMEM((4, 4, 192, 128), BF),
            pltpu.VMEM((4, 4, 64, 128), BF),
            pltpu.VMEM((8, 4, 64, 256), BF),
            pltpu.VMEM((8, 64, 8, 128), BF),
            pltpu.SemaphoreType.DMA((8,)),
        ],
        far_out=(0,),
    )


def solution(mesh):
    placed = (P("dp", "slab", "filt", None), P(), P(), P(), P(), P(), P())
    return jax.shard_map(
        lambda *args: tuple(per_device(*args)),
        mesh=mesh,
        in_specs=placed,
        out_specs=(P("dp", "slab", "filt", None), P("dp", "slab", "filt")),
        check_vma=False,
    )
```

```python
import jax
import jax.numpy as jnp
from jax import lax
from jax.experimental import pallas as pl
from jax.experimental.pallas import tpu as pltpu
from jax.sharding import PartitionSpec as P

BF = jnp.bfloat16
F32 = jnp.float32
VMEM = pl.BlockSpec(memory_space=pltpu.VMEM)
ANY = pl.BlockSpec(memory_space=pltpu.HBM)
TAPS = 9 * 64


def shape(*dims, kind=BF):
    return jax.ShapeDtypeStruct(dims, kind)


def kernel_call(body, name, flops, operands, outs, scratch=(), far_in=(), far_out=()):
    size = lambda s: s.size * s.dtype.itemsize
    moved = sum(size(s) for s in operands) + sum(size(s) for s in outs)
    return pl.pallas_call(
        body,
        name=name,
        out_shape=outs,
        in_specs=[ANY if i in far_in else VMEM for i in range(len(operands))],
        out_specs=[ANY if i in far_out else VMEM for i in range(len(outs))],
        scratch_shapes=list(scratch),
        compiler_params=pltpu.CompilerParams(vmem_limit_bytes=28 * 2**20),
        cost_estimate=pl.CostEstimate(flops=flops, bytes_accessed=moved, transcendentals=0),
    )(*operands)


def lrelu(values):
    return jnp.maximum(values, 0.01 * values)


def is_even():
    return lax.rem(lax.axis_index("filt"), 2) == 0


def shifted(dst, row):
    dst[0:64] = pltpu.roll(row, 1, 1)
    dst[64:128] = row
    dst[128:192] = pltpu.roll(row, 127, 1)


def stacked(block, z, y):
    return jnp.concatenate([block(z + d, y)[...] for d in (-1, 0, 1, 2)], axis=0)


def activated(sums):
    out = lrelu(sums).astype(BF)
    return out[0:64], out[64:128]


def conv_pair(block, z, rows, weight, bias):
    cells = jnp.concatenate(
        [jnp.concatenate([stacked(block, z, y + p) for p in (-1, 0, 1)], axis=0) for y in rows], axis=1
    )
    sums = jnp.dot(weight[...], cells, preferred_element_type=F32) + bias[...]
    parts = [activated(sums[:, 128 * j : 128 * j + 128]) for j in range(2)]
    return [(z + i, y, parts[j][i]) for i in range(2) for j, y in enumerate(rows)]


def tap_sum(block, z, weight, p, rows):
    cells = jnp.concatenate([stacked(block, z, y) for y in rows], axis=1)
    taps = weight[:, 4 * 192 * (p + 1) : 4 * 192 * (p + 2)]
    sums = jnp.dot(taps, cells, preferred_element_type=F32)
    return sums[:, 0:128], sums[:, 128:256]


def known_sums(block, z, s, weight, bias, dest):
    low, mid = tap_sum(block, z, weight, 1, (0 + s, 1 + s))
    mid_also, top = tap_sum(block, z, weight, 0, (0 + s, 7 - s))
    high, top_also = tap_sum(block, z, weight, -1, (7 - s, 6 - s))
    base = bias[:, 0:128]
    dest[0] = low + base
    dest[1] = mid + mid_also + base
    dest[2] = top + top_also + base
    dest[3] = high + base


def edge_rows(block, z, s, weight, known):
    low, high = tap_sum(block, z, weight, 0, (-1 + s, 8 - s))
    mid, low_also = tap_sum(block, z, weight, -1, (-1 + s, -2 + s))
    top, high_also = tap_sum(block, z, weight, 1, (8 - s, 9 - s))
    totals = (known[0] + low + low_also, known[1] + mid, known[2] + top, known[3] + high + high_also)
    parts = [activated(total) for total in totals]
    return [(z + i, y, parts[j][i]) for i in range(2) for j, y in enumerate((-1 + s, s, 7 - s, 8 - s))]


def split_kernel(vol, w0, w1, w2, w3, w4, w5, own, first, second, planes, v0, v1, v2, v3, v4, v5, held, sems):
    groups = [pl.ds(16 * g, 16) for g in range(4)]
    copies = [pltpu.make_async_copy(vol.at[g], held.at[g], sems.at[i]) for i, g in enumerate(groups)]
    copies += [
        pltpu.make_async_copy(a, b, sems.at[4 + i])
        for i, (a, b) in enumerate(((w0, v0), (w1, v1), (w2, v2), (w3, v3), (w4, v4), (w5, v5)))
    ]
    for copy in copies:
        copy.start()
    even = is_even()
    for i, g in enumerate(groups):
        copies[i].wait()
        for z in range(8):
            rows = jnp.swapaxes(held[g, z], 0, 1)
            own[z, :, g] = rows
            if z in CORNER_OF:
                planes[CORNER_OF[z], :, g] = rows
            first[z, :, g] = jnp.where(even, rows[6:8], rows[0:2])
            second[z, :, g] = jnp.where(even, rows[0:2], rows[6:8])
    for copy in copies[4:]:
        copy.wait()


def weight_kernel(first, first_bias, second, second_bias, third, third_bias, a1, a2, ad, b1, b2, bd, pick):
    eye = lax.broadcasted_iota(jnp.int32, (64, 64), 0) == lax.broadcasted_iota(jnp.int32, (64, 64), 1)
    unit = eye.astype(BF)

    def flipped(rows):
        return lax.dot_general(unit, rows, (((1,), (1,)), ((), ())), preferred_element_type=F32).astype(BF)

    def column(bias):
        spread = jnp.where(eye, jnp.broadcast_to(bias[...].reshape(1, 64), (64, 64)), 0.0)
        return jnp.broadcast_to(jnp.sum(spread, axis=1, keepdims=True), (64, 256))

    blank = jnp.zeros((192, 64), BF)
    for source, dest in ((first, a1), (second, a2)):
        piece = lambda a, p: source[9 * a + 3 * p : 9 * a + 3 * p + 3].reshape(192, 64)
        for zo in range(2):
            columns = [
                piece(zi - zo, p) if 0 <= zi - zo < 3 else blank for p in range(3) for zi in range(4)
            ]
            dest[64 * zo : 64 * zo + 64] = flipped(jnp.concatenate(columns, axis=0))
    ad[...] = flipped(third[...].reshape(512, 64))
    for source, dest in ((first_bias, b1), (second_bias, b2)):
        spread = column(source)
        dest[0:64] = spread
        dest[64:128] = spread
    bd[...] = column(third_bias)
    src = lax.broadcasted_iota(jnp.int32, (256, 256), 0)
    dst = lax.broadcasted_iota(jnp.int32, (256, 256), 1)
    half, cell = (dst // 64) % 2, dst % 64
    pick[...] = (src == half * 128 + 2 * cell + dst // 128).astype(F32).astype(BF)


CORNER_OF = {6: 0, 7: 1, 0: 2, 1: 3}
EDGE = {0: 0, 1: 1, 6: 2, 7: 3}
FAR = {-2: 0, -1: 1, 8: 2, 9: 3}
KEPT = {1: 0, 2: 1, 5: 2, 6: 3}
NEW = {-1: 0, 0: 1, 7: 2, 8: 3}
CORNER = {-2: 0, -1: 1, 8: 2, 9: 3}
SIDE = {-1: 0, 0: 1, 7: 2, 8: 3}


def inner_kernel(own, planes, a1, b1, a2, b2, kept, skip, sums1, sums2, vs, hs):
    def spot(z, y):
        return vs.at[z + 2, y]

    def hidden(z, y):
        return kept.at[z + 1, KEPT[y]] if y in KEPT else hs.at[z + 1, y - 3]

    for z in range(-2, 10):
        for y in range(8):
            shifted(spot(z, y), own[z, y] if 0 <= z < 8 else planes[CORNER[z], y])
    for z in range(-1, 9, 2):
        for y in (1, 3, 5):
            for zo, yo, row in conv_pair(spot, z, (y, y + 1), a1, b1):
                shifted(hidden(zo, yo), row)
    for z in range(-1, 9, 2):
        known_sums(spot, z, 0, a1, b1, sums1.at[(z + 1) // 2])
    for z in range(0, 8, 2):
        for y in (2, 4):
            for zo, yo, row in conv_pair(hidden, z, (y, y + 1), a2, b2):
                skip[zo, yo - 2] = row
    for z in range(0, 8, 2):
        known_sums(hidden, z, 1, a2, b2, sums2.at[z // 2])


def turned(rows):
    return jnp.swapaxes(rows, 0, 1)


def picked(rows, pick, dest):
    for y in range(2):
        wide = jnp.concatenate(
            [jnp.concatenate([rows[4 * y + j], rows[4 * y + j + 1]], axis=0) for j in (0, 2)], axis=1
        )
        chosen = jnp.dot(wide, pick[...], preferred_element_type=F32).astype(BF)
        for p in range(2):
            for q in range(2):
                dest[2 * p + q, :, 128 * y : 128 * y + 128] = chosen[64 * p : 64 * p + 64, 128 * q : 128 * q + 128]


def descended(cells, weight, bias):
    sums = jnp.dot(weight[...], cells.reshape(512, 256), preferred_element_type=F32)
    return lrelu(sums + bias[...]).astype(BF)


def middle_kernel(first, second, kept, mid, sums1, sums2, a1, a2, ad, bd, pick, far, fresh, held, coarse, part, cells):
    even = is_even()
    for z in range(8):
        for i in range(2):
            shifted(far.at[z, i], jnp.where(even, second[z, i], first[z, i]))
            shifted(far.at[z, 2 + i], jnp.where(even, first[z, i], second[z, i]))

    def spot(z, y):
        return far.at[z, FAR[y]]

    def hidden(z, y):
        return kept.at[z + 1, KEPT[y]] if y in KEPT else fresh.at[z - 1, NEW[y]]

    for z in (1, 3, 5):
        for zo, yo, row in edge_rows(spot, z, 0, a1, sums1.at[(z + 1) // 2]):
            shifted(hidden(zo, yo), row)
    for z in (2, 4):
        for zo, yo, row in edge_rows(hidden, z, 1, a2, sums2.at[z // 2]):
            part[zo - 2, EDGE[yo]] = row
        for k in (z - 2, z - 1):
            rows = jnp.stack([(part[k, EDGE[y]] if y in EDGE else mid[k + 2, y - 2]) for y in range(8)], axis=0)
            held[k] = turned(rows)
            picked(rows, pick, cells.at[k])
        coarse[z // 2 - 1] = descended(cells[z - 2 : z], ad, bd)


def outer_kernel(
    corners, far, kept, fresh, mid, held, half, sums1, sums2, a1, a2, ad, bd, pick, skip, coarse, near, side, ends, cells, last, small, sems
):
    always = lax.axis_index("filt") >= 0
    copies = [pltpu.make_async_copy(held.at[z - 2], skip.at[:, z], sems.at[z]) for z in range(2, 6)]

    @pl.when(always)
    def _():
        for copy in copies:
            copy.start()

    even = is_even()

    def spot(z, y):
        return near.at[CORNER[z], FAR[y]] if z in CORNER else far.at[z, FAR[y]]

    def hidden(z, y):
        if y in KEPT:
            return kept.at[z + 1, KEPT[y]]
        return side.at[SIDE[z], NEW[y]] if z in SIDE else fresh.at[z - 1, NEW[y]]

    def output(k):
        z = k if k < 2 else k + 4
        return pltpu.make_async_copy(last.at[k], skip.at[:, z], sems.at[z])

    for k in range(4):
        for i in range(2):
            shifted(near.at[k, i], jnp.where(even, corners[1, k, i], corners[0, k, i]))
            shifted(near.at[k, 2 + i], jnp.where(even, corners[0, k, i], corners[1, k, i]))
    for z in (-1, 7):
        for zo, yo, row in edge_rows(spot, z, 0, a1, sums1.at[(z + 1) // 2]):
            shifted(hidden(zo, yo), row)
    for z in (0, 6):
        for zo, yo, row in edge_rows(hidden, z, 1, a2, sums2.at[z // 2]):
            ends[zo if zo < 2 else zo - 4, EDGE[yo]] = row
    for k in range(4):
        z = k if k < 2 else k + 4
        rows = jnp.stack([(ends[k, EDGE[y]] if y in EDGE else mid[z, y - 2]) for y in range(8)], axis=0)
        last[k] = turned(rows)
        output(k).start()
        picked(rows, pick, cells.at[k])
    small[:, 1] = half[0]
    small[:, 2] = half[1]
    small[:, 0] = descended(cells[0:2], ad, bd)
    small[:, 3] = descended(cells[2:4], ad, bd)
    final = pltpu.make_async_copy(small, coarse, sems.at[8])
    final.start()
    for copy in copies:
        copy.wait()
    for k in range(4):
        output(k).wait()
    final.wait()


def per_device(volume, first_weight, first_bias, second_weight, second_bias, down_weight, down_bias):
    peers = lax.axis_size("filt")

    def pairs(begin):
        ways = [(i, (i + 1) % peers) for i in range(begin, peers, 2)]
        return ways + [(j, i) for i, j in ways]

    swap = [(0, 1), (1, 0)]
    raw = [first_weight, first_bias, second_weight, second_bias, down_weight, down_bias]
    operands = [pltpu.with_memory_space_constraint(a, pltpu.HBM) for a in [volume] + raw]
    own, first, second, planes, *raw = kernel_call(
        split_kernel, "split", 0, operands,
        [shape(8, 8, 64, 128), shape(8, 2, 64, 128), shape(8, 2, 64, 128), shape(4, 8, 64, 128)]
        + [shape(*a.shape, kind=a.dtype) for a in raw],
        [pltpu.VMEM((64, 8, 8, 128), BF), pltpu.SemaphoreType.DMA((10,))], far_in=range(7),
    )
    second = lax.ppermute(second, "filt", pairs(1))
    first = lax.ppermute(first, "filt", pairs(0))
    planes = lax.ppermute(planes, "slab", swap)
    a1, a2, ad, b1, b2, bd, pick = kernel_call(
        weight_kernel, "weights", 10**8,
        raw,
        [shape(128, 4 * TAPS), shape(128, 4 * TAPS), shape(64, 512), shape(128, 256, kind=F32), shape(128, 256, kind=F32), shape(64, 256, kind=F32), shape(256, 256)],
    )
    kept, mid, sums1, sums2 = kernel_call(
        inner_kernel, "inner", 4 * 10**9, [own, planes, a1, b1, a2, b2],
        [shape(10, 4, 192, 128), shape(8, 4, 64, 128), shape(5, 4, 128, 128, kind=F32), shape(4, 4, 128, 128, kind=F32)],
        [pltpu.VMEM((12, 8, 192, 128), BF), pltpu.VMEM((10, 2, 192, 128), BF)],
    )
    first, second, mid = lax.optimization_barrier((first, second, mid))
    edges = jnp.stack([jnp.concatenate([rows[6:8], rows[0:2]], axis=0) for rows in (first, second)], axis=0)
    corners = lax.ppermute(edges, "slab", swap)
    far, fresh, held, half = kernel_call(
        middle_kernel, "middle", 2 * 10**9, [first, second, kept, mid, sums1, sums2, a1, a2, ad, bd, pick],
        [shape(8, 4, 192, 128), shape(6, 4, 192, 128), shape(4, 64, 8, 128), shape(2, 64, 256)],
        [pltpu.VMEM((4, 4, 64, 128), BF), pltpu.VMEM((4, 4, 64, 256), BF)],
    )
    return kernel_call(
        outer_kernel, "outer", 2 * 10**9, [corners, far, kept, fresh, mid, held, half, sums1, sums2, a1, a2, ad, bd, pick],
        [shape(64, 8, 8, 128), shape(64, 4, 256)],
        [
            pltpu.VMEM((4, 4, 192, 128), BF),
            pltpu.VMEM((4, 4, 192, 128), BF),
            pltpu.VMEM((4, 4, 64, 128), BF),
            pltpu.VMEM((4, 4, 64, 256), BF),
            pltpu.VMEM((4, 64, 8, 128), BF),
            pltpu.VMEM((64, 4, 256), BF),
            pltpu.SemaphoreType.DMA((9,)),
        ],
        far_out=(0, 1),
    )


def solution(mesh):
    placed = (P("dp", "slab", "filt", None), P(), P(), P(), P(), P(), P())
    return jax.shard_map(
        lambda *args: tuple(per_device(*args)),
        mesh=mesh,
        in_specs=placed,
        out_specs=(P("dp", "slab", "filt", None), P("dp", "slab", "filt")),
        check_vma=False,
    )
```

```python
import jax
import jax.numpy as jnp
from jax import lax
from jax.experimental import pallas as pl
from jax.experimental.pallas import tpu as pltpu
from jax.sharding import PartitionSpec as P

BF = jnp.bfloat16
F32 = jnp.float32
VMEM = pl.BlockSpec(memory_space=pltpu.VMEM)
ANY = pl.BlockSpec(memory_space=pltpu.HBM)
TAPS = 9 * 64


def shape(*dims, kind=BF):
    return jax.ShapeDtypeStruct(dims, kind)


def kernel_call(body, name, flops, operands, outs, scratch=(), far_in=(), far_out=()):
    size = lambda s: s.size * s.dtype.itemsize
    moved = sum(size(s) for s in operands) + sum(size(s) for s in outs)
    return pl.pallas_call(
        body,
        name=name,
        out_shape=outs,
        in_specs=[ANY if i in far_in else VMEM for i in range(len(operands))],
        out_specs=[ANY if i in far_out else VMEM for i in range(len(outs))],
        scratch_shapes=list(scratch),
        compiler_params=pltpu.CompilerParams(vmem_limit_bytes=28 * 2**20),
        cost_estimate=pl.CostEstimate(flops=flops, bytes_accessed=moved, transcendentals=0),
    )(*operands)


def lrelu(values):
    return jnp.maximum(values, 0.01 * values)


def is_even():
    return lax.rem(lax.axis_index("filt"), 2) == 0


def shifted(dst, row):
    dst[0:64] = pltpu.roll(row, 1, 1)
    dst[64:128] = row
    dst[128:192] = pltpu.roll(row, 127, 1)


def stacked(block, z, y):
    return jnp.concatenate([block(z + d, y)[...] for d in (-1, 0, 1, 2)], axis=0)


def activated(sums):
    out = lrelu(sums).astype(BF)
    return out[0:64], out[64:128]


def conv_pair(block, z, rows, weight, bias):
    cells = jnp.concatenate(
        [jnp.concatenate([stacked(block, z, y + p) for p in (-1, 0, 1)], axis=0) for y in rows], axis=1
    )
    sums = jnp.dot(weight[...], cells, preferred_element_type=F32) + bias[...]
    parts = [activated(sums[:, 128 * j : 128 * j + 128]) for j in range(2)]
    return [(z + i, y, parts[j][i]) for i in range(2) for j, y in enumerate(rows)]


def tap_sum(block, z, weight, p, rows):
    cells = jnp.concatenate([stacked(block, z, y) for y in rows], axis=1)
    taps = weight[:, 4 * 192 * (p + 1) : 4 * 192 * (p + 2)]
    sums = jnp.dot(taps, cells, preferred_element_type=F32)
    return sums[:, 0:128], sums[:, 128:256]


def known_sums(block, z, s, weight, bias, dest):
    low, mid = tap_sum(block, z, weight, 1, (0 + s, 1 + s))
    mid_also, top = tap_sum(block, z, weight, 0, (0 + s, 7 - s))
    high, top_also = tap_sum(block, z, weight, -1, (7 - s, 6 - s))
    base = bias[:, 0:128]
    dest[0] = low + base
    dest[1] = mid + mid_also + base
    dest[2] = top + top_also + base
    dest[3] = high + base


def edge_rows(block, z, s, weight, known):
    low, high = tap_sum(block, z, weight, 0, (-1 + s, 8 - s))
    mid, low_also = tap_sum(block, z, weight, -1, (-1 + s, -2 + s))
    top, high_also = tap_sum(block, z, weight, 1, (8 - s, 9 - s))
    totals = (known[0] + low + low_also, known[1] + mid, known[2] + top, known[3] + high + high_also)
    parts = [activated(total) for total in totals]
    return [(z + i, y, parts[j][i]) for i in range(2) for j, y in enumerate((-1 + s, s, 7 - s, 8 - s))]


def split_kernel(vol, own, first, second, planes, held, sems):
    groups = [pl.ds(16 * g, 16) for g in range(4)]
    copies = [pltpu.make_async_copy(vol.at[g], held.at[g], sems.at[i]) for i, g in enumerate(groups)]
    for copy in copies:
        copy.start()
    even = is_even()
    for i, g in enumerate(groups):
        copies[i].wait()
        for z in range(8):
            rows = jnp.swapaxes(held[g, z], 0, 1)
            own[z, :, g] = rows
            if z in CORNER_OF:
                planes[CORNER_OF[z], :, g] = rows
            first[z, :, g] = jnp.where(even, rows[0:2], rows[6:8])
            second[z, :, g] = jnp.where(even, rows[6:8], rows[0:2])


def weight_kernel(w0, w1, w2, w3, w4, w5, a1, a2, ad, b1, b2, bd, pick, first, first_bias, second, second_bias, third, third_bias, sems):
    copies = [
        pltpu.make_async_copy(a, b, sems.at[i])
        for i, (a, b) in enumerate(((w0, first), (w1, first_bias), (w2, second), (w3, second_bias), (w4, third), (w5, third_bias)))
    ]
    for copy in copies:
        copy.start()
    for copy in copies:
        copy.wait()
    eye = lax.broadcasted_iota(jnp.int32, (64, 64), 0) == lax.broadcasted_iota(jnp.int32, (64, 64), 1)
    unit = eye.astype(BF)

    def flipped(rows):
        return lax.dot_general(unit, rows, (((1,), (1,)), ((), ())), preferred_element_type=F32).astype(BF)

    def column(bias):
        spread = jnp.where(eye, jnp.broadcast_to(bias[...].reshape(1, 64), (64, 64)), 0.0)
        return jnp.broadcast_to(jnp.sum(spread, axis=1, keepdims=True), (64, 256))

    blank = jnp.zeros((192, 64), BF)
    for source, dest in ((first, a1), (second, a2)):
        piece = lambda a, p: source[9 * a + 3 * p : 9 * a + 3 * p + 3].reshape(192, 64)
        for zo in range(2):
            columns = [
                piece(zi - zo, p) if 0 <= zi - zo < 3 else blank for p in range(3) for zi in range(4)
            ]
            dest[64 * zo : 64 * zo + 64] = flipped(jnp.concatenate(columns, axis=0))
    ad[...] = flipped(third[...].reshape(512, 64))
    for source, dest in ((first_bias, b1), (second_bias, b2)):
        spread = column(source)
        dest[0:64] = spread
        dest[64:128] = spread
    bd[...] = column(third_bias)
    src = lax.broadcasted_iota(jnp.int32, (256, 256), 0)
    dst = lax.broadcasted_iota(jnp.int32, (256, 256), 1)
    half, cell = (dst // 64) % 2, dst % 64
    pick[...] = (src == half * 128 + 2 * cell + dst // 128).astype(F32).astype(BF)


CORNER_OF = {6: 0, 7: 1, 0: 2, 1: 3}
EDGE = {0: 0, 1: 1, 6: 2, 7: 3}
FAR = {-2: 0, -1: 1, 8: 2, 9: 3}
KEPT = {1: 0, 2: 1, 5: 2, 6: 3}
NEW = {-1: 0, 0: 1, 7: 2, 8: 3}
CORNER = {-2: 0, -1: 1, 8: 2, 9: 3}
SIDE = {-1: 0, 0: 1, 7: 2, 8: 3}


def inner_kernel(own, planes, a1, b1, a2, b2, kept, skip, sums1, sums2, vs, hs):
    def spot(z, y):
        return vs.at[z + 2, y]

    def hidden(z, y):
        return kept.at[z + 1, KEPT[y]] if y in KEPT else hs.at[z + 1, y - 3]

    for z in range(-2, 10):
        for y in range(8):
            shifted(spot(z, y), own[z, y] if 0 <= z < 8 else planes[CORNER[z], y])
    for z in range(-1, 9, 2):
        for y in (1, 3, 5):
            for zo, yo, row in conv_pair(spot, z, (y, y + 1), a1, b1):
                shifted(hidden(zo, yo), row)
    for z in range(-1, 9, 2):
        known_sums(spot, z, 0, a1, b1, sums1.at[(z + 1) // 2])
    for z in range(0, 8, 2):
        for y in (2, 4):
            for zo, yo, row in conv_pair(hidden, z, (y, y + 1), a2, b2):
                skip[zo, yo - 2] = row
    for z in range(0, 8, 2):
        known_sums(hidden, z, 1, a2, b2, sums2.at[z // 2])


def turned(rows):
    return jnp.swapaxes(rows, 0, 1)


def picked(rows, pick, dest):
    for y in range(2):
        wide = jnp.concatenate(
            [jnp.concatenate([rows[4 * y + j], rows[4 * y + j + 1]], axis=0) for j in (0, 2)], axis=1
        )
        chosen = jnp.dot(wide, pick[...], preferred_element_type=F32).astype(BF)
        for p in range(2):
            for q in range(2):
                dest[2 * p + q, :, 128 * y : 128 * y + 128] = chosen[64 * p : 64 * p + 64, 128 * q : 128 * q + 128]


def descended(cells, weight, bias):
    sums = jnp.dot(weight[...], cells.reshape(512, 256), preferred_element_type=F32)
    return lrelu(sums + bias[...]).astype(BF)


def middle_kernel(first, second, kept, mid, sums1, sums2, a1, a2, ad, bd, pick, far, fresh, held, coarse, part, cells):
    even = is_even()
    for z in range(8):
        for i in range(2):
            shifted(far.at[z, i], jnp.where(even, first[z, i], second[z, i]))
            shifted(far.at[z, 2 + i], jnp.where(even, second[z, i], first[z, i]))

    def spot(z, y):
        return far.at[z, FAR[y]]

    def hidden(z, y):
        return kept.at[z + 1, KEPT[y]] if y in KEPT else fresh.at[z - 1, NEW[y]]

    for z in (1, 3, 5):
        for zo, yo, row in edge_rows(spot, z, 0, a1, sums1.at[(z + 1) // 2]):
            shifted(hidden(zo, yo), row)
    for z in (2, 4):
        for zo, yo, row in edge_rows(hidden, z, 1, a2, sums2.at[z // 2]):
            part[zo - 2, EDGE[yo]] = row
        for k in (z - 2, z - 1):
            rows = jnp.stack([(part[k, EDGE[y]] if y in EDGE else mid[k + 2, y - 2]) for y in range(8)], axis=0)
            held[k] = turned(rows)
            picked(rows, pick, cells.at[k])
        coarse[z // 2 - 1] = descended(cells[z - 2 : z], ad, bd)


def outer_kernel(
    corners, far, kept, fresh, mid, held, half, sums1, sums2, a1, a2, ad, bd, pick, skip, coarse, near, side, ends, cells, last, small, sems
):
    always = lax.axis_index("filt") >= 0
    copies = [pltpu.make_async_copy(held.at[z - 2], skip.at[:, z], sems.at[z]) for z in range(2, 6)]

    @pl.when(always)
    def _():
        for copy in copies:
            copy.start()

    even = is_even()

    def spot(z, y):
        return near.at[CORNER[z], FAR[y]] if z in CORNER else far.at[z, FAR[y]]

    def hidden(z, y):
        if y in KEPT:
            return kept.at[z + 1, KEPT[y]]
        return side.at[SIDE[z], NEW[y]] if z in SIDE else fresh.at[z - 1, NEW[y]]

    def output(k):
        z = k if k < 2 else k + 4
        return pltpu.make_async_copy(last.at[k], skip.at[:, z], sems.at[z])

    for k in range(4):
        for i in range(2):
            shifted(near.at[k, i], jnp.where(even, corners[0, k, i], corners[1, k, i]))
            shifted(near.at[k, 2 + i], jnp.where(even, corners[1, k, i], corners[0, k, i]))
    for z in (-1, 7):
        for zo, yo, row in edge_rows(spot, z, 0, a1, sums1.at[(z + 1) // 2]):
            shifted(hidden(zo, yo), row)
    for z in (0, 6):
        for zo, yo, row in edge_rows(hidden, z, 1, a2, sums2.at[z // 2]):
            ends[zo if zo < 2 else zo - 4, EDGE[yo]] = row
    for k in range(4):
        z = k if k < 2 else k + 4
        rows = jnp.stack([(ends[k, EDGE[y]] if y in EDGE else mid[z, y - 2]) for y in range(8)], axis=0)
        last[k] = turned(rows)
        output(k).start()
        picked(rows, pick, cells.at[k])
    small[:, 1] = half[0]
    small[:, 2] = half[1]
    small[:, 0] = descended(cells[0:2], ad, bd)
    small[:, 3] = descended(cells[2:4], ad, bd)
    final = pltpu.make_async_copy(small, coarse, sems.at[8])
    final.start()
    for copy in copies:
        copy.wait()
    for k in range(4):
        output(k).wait()
    final.wait()


def per_device(volume, first_weight, first_bias, second_weight, second_bias, down_weight, down_bias):
    peers = lax.axis_size("filt")

    def pairs(begin):
        ways = [(i, (i + 1) % peers) for i in range(begin, peers, 2)]
        return ways + [(j, i) for i, j in ways]

    swap = [(0, 1), (1, 0)]
    raw = [first_weight, first_bias, second_weight, second_bias, down_weight, down_bias]
    volume, *raw = [pltpu.with_memory_space_constraint(a, pltpu.HBM) for a in [volume] + raw]
    own, first, second, planes = kernel_call(
        split_kernel, "split", 0, [volume],
        [shape(8, 8, 64, 128), shape(8, 2, 64, 128), shape(8, 2, 64, 128), shape(4, 8, 64, 128)],
        [pltpu.VMEM((64, 8, 8, 128), BF), pltpu.SemaphoreType.DMA((4,))], far_in=(0,),
    )
    second = lax.ppermute(second, "filt", pairs(0))
    first = lax.ppermute(first, "filt", pairs(1))
    planes = lax.ppermute(planes, "slab", swap)
    a1, a2, ad, b1, b2, bd, pick = kernel_call(
        weight_kernel, "weights", 10**8,
        raw,
        [shape(128, 4 * TAPS), shape(128, 4 * TAPS), shape(64, 512), shape(128, 256, kind=F32), shape(128, 256, kind=F32), shape(64, 256, kind=F32), shape(256, 256)],
        [pltpu.VMEM(a.shape, a.dtype) for a in raw] + [pltpu.SemaphoreType.DMA((6,))], far_in=range(6),
    )
    kept, mid, sums1, sums2 = kernel_call(
        inner_kernel, "inner", 4 * 10**9, [own, planes, a1, b1, a2, b2],
        [shape(10, 4, 192, 128), shape(8, 4, 64, 128), shape(5, 4, 128, 128, kind=F32), shape(4, 4, 128, 128, kind=F32)],
        [pltpu.VMEM((12, 8, 192, 128), BF), pltpu.VMEM((10, 2, 192, 128), BF)],
    )
    first, second, mid = lax.optimization_barrier((first, second, mid))
    edges = jnp.stack([jnp.concatenate([rows[6:8], rows[0:2]], axis=0) for rows in (first, second)], axis=0)
    corners = lax.ppermute(edges, "slab", swap)
    far, fresh, held, half = kernel_call(
        middle_kernel, "middle", 2 * 10**9, [first, second, kept, mid, sums1, sums2, a1, a2, ad, bd, pick],
        [shape(8, 4, 192, 128), shape(6, 4, 192, 128), shape(4, 64, 8, 128), shape(2, 64, 256)],
        [pltpu.VMEM((4, 4, 64, 128), BF), pltpu.VMEM((4, 4, 64, 256), BF)],
    )
    return kernel_call(
        outer_kernel, "outer", 2 * 10**9, [corners, far, kept, fresh, mid, held, half, sums1, sums2, a1, a2, ad, bd, pick],
        [shape(64, 8, 8, 128), shape(64, 4, 256)],
        [
            pltpu.VMEM((4, 4, 192, 128), BF),
            pltpu.VMEM((4, 4, 192, 128), BF),
            pltpu.VMEM((4, 4, 64, 128), BF),
            pltpu.VMEM((4, 4, 64, 256), BF),
            pltpu.VMEM((4, 64, 8, 128), BF),
            pltpu.VMEM((64, 4, 256), BF),
            pltpu.SemaphoreType.DMA((9,)),
        ],
        far_out=(0, 1),
    )


def solution(mesh):
    placed = (P("dp", "slab", "filt", None), P(), P(), P(), P(), P(), P())
    return jax.shard_map(
        lambda *args: tuple(per_device(*args)),
        mesh=mesh,
        in_specs=placed,
        out_specs=(P("dp", "slab", "filt", None), P("dp", "slab", "filt")),
        check_vma=False,
    )
```
